32 devices in a mesh: dp: 8 (over y, x, core), tensor: 4 (over z).
Axes of the slice: x: 2, y: 2, z: 4, core: 2. Of those that a mesh axis runs over, the one named last changes fastest.
Arguments:
- tokens: bfloat16 [2048, 8192], P('dp'), may hold values from -6 to 6
- router_weight: bfloat16 [8192, 8], replicated, may hold values from -0.0625 to 0.0625
- gate_weight: bfloat16 [14336, 8192], P(('dp', 'tensor')), may hold values from -0.0625 to 0.0625
- up_weight: bfloat16 [14336, 8192], P(('dp', 'tensor')), may hold values from -0.0625 to 0.0625
- down_weight: bfloat16 [14336, 8192], P(('dp', 'tensor')), may hold values from -0.125 to 0.125
- cluster_of: int32 [14336, 1], P('dp'), may hold values from 0 to 7; in each aligned block of 1792 rows (0 to 1791, 1792 to 3583, ...) at most 448 rows name the same one
- expert_ids: int32 [2048, 2], P('dp'), may hold values from 0 to 7, all different within a row; in each aligned block of 256 rows (0 to 255, 256 to 511, ...) at most 128 rows name the same one
Outputs:
- mixed_out: bfloat16 [2048, 8192], P('dp', 'tensor')
The draws below stay inside these ranges and needn't reach their ends.
Inputs may be any that keep to these rules, and one draw needn't show every extreme that they name: `expert_ids`: in each aligned block of 256 rows (the tokens of one dp index) no expert is named by more than 128 rows, a bound that some block reaches; a row names two different experts; every expert is named somewhere. `cluster_of`: in each aligned block of 1792 hidden units no cluster holds more than 448 units, and some cluster holds exactly 448; every cluster holds some unit.
All inputs are finite; a program needn't handle non-finite values.
Results may differ from the reference program's by a relative error of at most 0.023.
Values may be sent and summed in bfloat16 or wider, within the bound.
A program may use at most 192 MiB of HBM per device.

```python
import math
import jax
import jax.numpy as jnp
import numpy as np
from jax import lax

D = 8192
FF = 14336
TOK_DP = 256
EXPERTS = 8
CAP = 128
UCAP = 448
TOKENS = 2048
N_DP = 8
N_TENSOR = 4


def levels(rng, extent, cuts, smallest, top_value):
    factor_of, own = 1.0, jax.random.fold_in(rng, 6)
    for dim, blocks in cuts:
        steps = jnp.exp(jax.random.uniform(jax.random.fold_in(own, dim), (blocks,), jnp.float32, smallest / len(cuts), top_value / len(cuts)))
        factor_of = factor_of * jnp.repeat(steps, extent[dim] // blocks).reshape([-1 if axis == dim else 1 for axis in range(len(extent))])
    return factor_of


def shared_out(key, own, number, rows, count, top, reach, skew):
    ranking = jax.random.permutation(key, count)
    heavy_load, common = load_shares(count, rows * top, reach, skew, True), load_shares(count, rows * top, reach, skew, False)
    places = jnp.arange(count)

    def named(lengths, offset_by):
        used = int((lengths > 0).sum())
        fixed = max(1, used // 4)
        shifted = fixed + (places - fixed + offset_by * (used - fixed)) % max(1, count - fixed)
        return jnp.zeros((count,), jnp.int32).at[ranking[jnp.where(places < fixed, places, shifted)]].set(jnp.asarray(lengths, jnp.int32))

    lengths = jnp.where(number % 4 == 0, named(heavy_load, number // 4), named(common, number - number // 4 - 1))
    mixed = jax.random.permutation(jax.random.fold_in(own, 3), count)
    source_of, sink = mixed[0:count // 2 * 2:2], mixed[1:count // 2 * 2:2]
    margin = jnp.minimum(lengths[source_of] - 1, reach - lengths[sink]) // 2
    margin = jnp.where((source_of == ranking[0]) | (sink == ranking[0]) | (lengths[sink] == 0), 0, jnp.maximum(margin, 0))
    shifted = jax.random.randint(jax.random.fold_in(own, 4), (count // 2,), 0, 1 << 20) % (margin + 1)
    lengths = lengths.at[source_of].add(-shifted).at[sink].add(shifted)
    labels = jnp.searchsorted(jnp.cumsum(lengths), jnp.arange(rows * top), side="right").astype(jnp.int32)
    grid = labels.reshape(top, rows).T
    grid = grid[jax.random.permutation(jax.random.fold_in(own, 1), rows)]
    offset_by = jax.random.randint(jax.random.fold_in(own, 2), (rows, 1), 0, top)
    return jnp.take_along_axis(grid, (jnp.arange(top)[None, :] + offset_by) % top, axis=1)


def load_shares(number_of, total, bound, slope, full):
    portions = [(1 << 20) // math.isqrt(standing ** slope) + 1 for standing in range(1, number_of + 1)]
    largest = bound if full else min(bound, max(-(-total // number_of), total * portions[0] // sum(portions)))
    least = 1 if total - largest >= number_of - 1 else 0
    counts, surplus = [largest] + [least] * (number_of - 1), total - largest - least * (number_of - 1)
    while surplus > 0:
        free = [i for i in range(1, number_of) if counts[i] < largest] or [i for i in range(1, number_of) if counts[i] < bound]
        mass, budget = sum([portions[i] for i in free]), surplus
        for i in free:
            extra = min(bound - counts[i], max(1, budget * portions[i] // mass), surplus)
            counts[i] = counts[i] + extra
            surplus = surplus - extra
    return np.array(counts)


def gaussian(key, dims, deviation, bound, cuts=(), dtype=jnp.bfloat16):
    values = jax.random.normal(key, dims, jnp.float32) * deviation
    if len(cuts) > 0:
        values = levels(key, dims, cuts, -0.22, 0.18) * values
    return jnp.clip(values, min=-bound, max=bound).astype(dtype)


def setup_inputs(seed: int = 0) -> dict:
    streams_of = jax.random.split(jax.random.key(seed), 8)
    tokens = gaussian(streams_of[0], (TOKENS, D), 1.0, 6.0, ((0, 8),))
    router_weight = gaussian(streams_of[1], (D, EXPERTS), D ** -0.5, 0.0625)
    gate_weight = gaussian(streams_of[2], (FF, D), D ** -0.5, 0.0625, ((0, 32),))
    up_weight = gaussian(streams_of[3], (FF, D), D ** -0.5, 0.0625, ((0, 32),))
    down_weight = gaussian(streams_of[4], (FF, D), (FF // EXPERTS) ** -0.5, 0.125, ((0, 32),))
    cluster_of_keys = jax.random.split(jax.random.fold_in(streams_of[5], 1), FF // (FF // N_DP))
    cluster_of_turns = jax.random.permutation(jax.random.fold_in(streams_of[5], 3), FF // (FF // N_DP))
    cluster_of = jax.vmap(lambda own, number: shared_out(jax.random.fold_in(streams_of[5], 2), own, number, FF // N_DP, EXPERTS, 1, UCAP, 1))(cluster_of_keys, cluster_of_turns).reshape((FF, 1))
    expert_ids_keys = jax.random.split(jax.random.fold_in(streams_of[6], 1), TOKENS // TOK_DP)
    expert_ids_turns = jax.random.permutation(jax.random.fold_in(streams_of[6], 3), TOKENS // TOK_DP)
    expert_ids = jax.vmap(lambda own, number: shared_out(jax.random.fold_in(streams_of[6], 2), own, number, TOK_DP, EXPERTS, 2, CAP, 2))(expert_ids_keys, expert_ids_turns).reshape((TOKENS, 2))
    return {"tokens": tokens, "router_weight": router_weight, "gate_weight": gate_weight, "up_weight": up_weight, "down_weight": down_weight, "cluster_of": cluster_of, "expert_ids": expert_ids}


def against(left_side, right_side):
    return lax.dot_general(left_side, right_side, (((1,), (1,)), ((), ())), preferred_element_type=jnp.float32)


def reference(tokens, router_weight, gate_weight, up_weight, down_weight, cluster_of, expert_ids):
    width_part = D // N_TENSOR
    logits = jnp.dot(tokens, router_weight, preferred_element_type=jnp.float32)
    scores = jax.nn.sigmoid(jnp.take_along_axis(logits, expert_ids, axis=1))
    mixing = scores / jnp.sum(scores, axis=1, keepdims=True)
    unit_cluster = cluster_of[:, 0]
    block_rows = 512 if TOKENS % 512 == 0 else TOKENS
    count_blocks = TOKENS // block_rows

    def one_block(inputs):
        token_block, id_block, mix_block = inputs
        gate_sum = jnp.zeros((block_rows, FF), jnp.float32)
        up_sum = jnp.zeros((block_rows, FF), jnp.float32)
        for block_index in range(N_TENSOR):
            lower = block_index * width_part
            piece = token_block[:, lower:lower + width_part]
            gate_term = against(piece, gate_weight[:, lower:lower + width_part]).astype(jnp.bfloat16)
            up_term = against(piece, up_weight[:, lower:lower + width_part]).astype(jnp.bfloat16)
            gate_sum = gate_sum + lax.optimization_barrier(gate_term).astype(jnp.float32)
            up_sum = up_sum + lax.optimization_barrier(up_term).astype(jnp.float32)
        hidden = (jax.nn.silu(gate_sum) * up_sum).astype(jnp.bfloat16)
        total = jnp.zeros((block_rows, D), jnp.float32)
        for slot_index in range(2):
            keep = unit_cluster[None, :] == id_block[:, slot_index:slot_index + 1]
            masked = jnp.where(keep, hidden, jnp.zeros_like(hidden))
            expert_out = jnp.dot(masked, down_weight, preferred_element_type=jnp.float32).astype(jnp.bfloat16)
            total = total + mix_block[:, slot_index:slot_index + 1] * lax.optimization_barrier(expert_out).astype(jnp.float32)
        return total.astype(jnp.bfloat16)

    outputs = lax.map(one_block, (tokens.reshape(count_blocks, block_rows, D),
                                  expert_ids.reshape(count_blocks, block_rows, 2),
                                  mixing.reshape(count_blocks, block_rows, 2)))
    return outputs.reshape(TOKENS, D)
```

```python
import jax
import jax.numpy as jnp
from jax import lax
from jax.sharding import PartitionSpec as P

CHUNK_TOKENS = 512


def against(left_side, right_side):
    return lax.dot_general(
        left_side, right_side, (((1,), (1,)), ((), ())), preferred_element_type=jnp.float32
    )


def on_device(tokens, router_weight, gate_weight, up_weight, down_weight, cluster_of, expert_ids):
    owners = lax.axis_size("dp")
    experts = router_weight.shape[1]
    units = gate_weight.shape[0]
    token_count = tokens.shape[0]
    same_core = [list(range(core, owners, 2)) for core in range(2)]
    swap = [(i, i ^ 1) for i in range(owners)]

    own_cluster = lax.dynamic_slice_in_dim(
        cluster_of[:, 0], lax.axis_index("tensor") * units, units, 0
    ).astype(jnp.float32)
    cluster = jnp.concatenate([own_cluster, lax.ppermute(own_cluster, "dp", swap)])
    gate_peer = lax.ppermute(gate_weight, "dp", swap)
    up_peer = lax.ppermute(up_weight, "dp", swap)
    down_peer = lax.ppermute(down_weight, "dp", swap)

    expert_range = jnp.arange(experts, dtype=jnp.int32)
    logits = jnp.dot(tokens, router_weight, preferred_element_type=jnp.float32)
    scores = jax.nn.sigmoid(jnp.take_along_axis(logits, expert_ids, axis=1))
    mixing = scores / jnp.sum(scores, axis=1, keepdims=True)
    shares = jnp.sum(
        jnp.where(expert_ids[:, :, None] == expert_range, mixing[:, :, None], 0.0), axis=1
    )
    unit_onehot = (cluster[None, :] == expert_range.astype(jnp.float32)[:, None]).astype(jnp.float32)

    chunk_count = max(1, token_count * (owners // 2) // CHUNK_TOKENS)
    rows = token_count // chunk_count
    results = []
    down_all = jnp.concatenate([down_weight, down_peer], axis=0)
    for chunk in range(chunk_count):
        piece = tokens[chunk * rows:(chunk + 1) * rows]
        share = shares[chunk * rows:(chunk + 1) * rows]
        if chunk >= 2:
            piece, share, results[-2] = lax.optimization_barrier((piece, share, results[-2]))
        gathered = lax.all_gather(piece, "dp", axis_index_groups=same_core, tiled=True)
        share_all = lax.all_gather(share, "dp", axis_index_groups=same_core, tiled=True)
        scale = jnp.dot(share_all, unit_onehot, precision=lax.Precision.HIGHEST)
        halves = []
        for part, (gate, up) in enumerate(((gate_weight, up_weight), (gate_peer, up_peer))):
            hidden = jax.nn.silu(against(gathered, gate)) * against(gathered, up)
            hidden = hidden * scale[:, part * units:(part + 1) * units]
            halves.append(hidden.astype(jnp.bfloat16))
        hidden = jnp.concatenate(halves, axis=1)
        partial = jnp.dot(hidden, down_all, preferred_element_type=jnp.float32).astype(jnp.bfloat16)
        summed = lax.psum_scatter(
            partial, "dp", scatter_dimension=0, axis_index_groups=same_core, tiled=True
        )
        results.append(lax.psum_scatter(summed, "tensor", scatter_dimension=1, tiled=True))
    return jnp.concatenate(results, axis=0)


def solution(mesh):
    in_specs = (
        P("dp", None),
        P(),
        P(("dp", "tensor"), None),
        P(("dp", "tensor"), None),
        P(("dp", "tensor"), None),
        P("dp", None),
        P("dp", None),
    )
    return jax.shard_map(
        on_device, mesh=mesh, in_specs=in_specs, out_specs=P("dp", "tensor"), check_vma=False
    )
```

```python
import jax
import jax.numpy as jnp
from jax import lax
from jax.sharding import PartitionSpec as P

CHUNK_TOKENS = 512


def against(left_side, right_side):
    return lax.dot_general(
        left_side, right_side, (((1,), (1,)), ((), ())), preferred_element_type=jnp.float32
    )


def swapped(array, step):
    return lax.ppermute(array, "dp", [(i, i ^ step) for i in range(lax.axis_size("dp"))])


def gather_square(piece):
    from_x, from_y = swapped(piece, 2), swapped(piece, 4)
    half = piece.shape[0] // 2
    across = [swapped(from_x[:half], 4), swapped(from_y[half:], 2)]
    return jnp.concatenate([piece, from_x, from_y] + across, axis=0)


def added(first, second):
    return (first.astype(jnp.float32) + second.astype(jnp.float32)).astype(jnp.bfloat16)


def scatter_square(partial):
    rows, half = partial.shape[0] // 4, partial.shape[1] // 2
    results = []
    for part, (first, second) in enumerate(((2, 4), (4, 2))):
        block = partial[:, part * half:(part + 1) * half].reshape(4, rows, half)
        near, far = (1, 2) if first == 2 else (2, 1)
        own_sum = added(block[0], swapped(block[near], first))
        far_sum = added(block[far], swapped(block[3], first))
        results.append(added(own_sum, swapped(far_sum, second)))
    return jnp.concatenate(results, axis=1)


def scatter_line(summed):
    count, here = lax.axis_size("tensor"), lax.axis_index("tensor")
    width = summed.shape[1] // count

    def block_of(index):
        return lax.dynamic_slice_in_dim(summed, lax.rem(index, count) * width, width, 1)

    total = block_of(here).astype(jnp.float32)
    for step in range(1, count):
        pairs = [(i, (i + step) % count) for i in range(count)]
        total = total + lax.ppermute(block_of(here + step), "tensor", pairs).astype(jnp.float32)
    return total.astype(jnp.bfloat16)


def on_device(tokens, router_weight, gate_weight, up_weight, down_weight, cluster_of, expert_ids):
    owners = lax.axis_size("dp")
    experts = router_weight.shape[1]
    units = gate_weight.shape[0]
    token_count = tokens.shape[0]
    same_core = [list(range(core, owners, 2)) for core in range(2)]
    swap = [(i, i ^ 1) for i in range(owners)]

    own_cluster = lax.dynamic_slice_in_dim(
        cluster_of[:, 0], lax.axis_index("tensor") * units, units, 0
    ).astype(jnp.float32)
    cluster = jnp.concatenate([own_cluster, lax.ppermute(own_cluster, "dp", swap)])
    gate_peer = lax.ppermute(gate_weight, "dp", swap)
    up_peer = lax.ppermute(up_weight, "dp", swap)
    down_peer = lax.ppermute(down_weight, "dp", swap)

    expert_range = jnp.arange(experts, dtype=jnp.int32)
    logits = jnp.dot(tokens, router_weight, preferred_element_type=jnp.float32)
    scores = jax.nn.sigmoid(jnp.take_along_axis(logits, expert_ids, axis=1))
    mixing = scores / jnp.sum(scores, axis=1, keepdims=True)
    shares = jnp.sum(
        jnp.where(expert_ids[:, :, None] == expert_range, mixing[:, :, None], 0.0), axis=1
    )
    unit_onehot = (cluster[None, :] == expert_range.astype(jnp.float32)[:, None]).astype(jnp.float32)

    chunk_count = max(1, token_count * (owners // 2) // CHUNK_TOKENS)
    rows = token_count // chunk_count
    square = owners == 8
    results = []
    down_all = jnp.concatenate([down_weight, down_peer], axis=0)
    for chunk in range(chunk_count):
        piece = tokens[chunk * rows:(chunk + 1) * rows]
        share = shares[chunk * rows:(chunk + 1) * rows]
        if chunk >= 2:
            piece, share, results[-2] = lax.optimization_barrier((piece, share, results[-2]))
        if square:
            gathered, share_all = gather_square(piece), gather_square(share)
        else:
            gathered = lax.all_gather(piece, "dp", axis_index_groups=same_core, tiled=True)
            share_all = lax.all_gather(share, "dp", axis_index_groups=same_core, tiled=True)
        scale = jnp.dot(share_all, unit_onehot, precision=lax.Precision.HIGHEST)
        halves = []
        for part, (gate, up) in enumerate(((gate_weight, up_weight), (gate_peer, up_peer))):
            hidden = jax.nn.silu(against(gathered, gate)) * against(gathered, up)
            hidden = hidden * scale[:, part * units:(part + 1) * units]
            halves.append(hidden.astype(jnp.bfloat16))
        hidden = jnp.concatenate(halves, axis=1)
        partial = jnp.dot(hidden, down_all, preferred_element_type=jnp.float32).astype(jnp.bfloat16)
        if square:
            results.append(scatter_line(scatter_square(partial)))
            continue
        summed = lax.psum_scatter(
            partial, "dp", scatter_dimension=0, axis_index_groups=same_core, tiled=True
        )
        results.append(lax.psum_scatter(summed, "tensor", scatter_dimension=1, tiled=True))
    return jnp.concatenate(results, axis=0)


def solution(mesh):
    in_specs = (
        P("dp", None),
        P(),
        P(("dp", "tensor"), None),
        P(("dp", "tensor"), None),
        P(("dp", "tensor"), None),
        P("dp", None),
        P("dp", None),
    )
    return jax.shard_map(
        on_device, mesh=mesh, in_specs=in_specs, out_specs=P("dp", "tensor"), check_vma=False
    )
```
